32 devices in a mesh: clips: 2 (over y), frame: 4 (over z), rows: 2 (over x), view: 2 (over core).
Axes of the slice: x: 2, y: 2, z: 4, core: 2. Of those that a mesh axis runs over, the one named last changes fastest.
Arguments:
- feats: bfloat16 [4, 4, 8, 480, 256], P(('clips', 'view'), 'frame', 'rows'), parts along dimension 0, may hold values from -8 to 8
- norm_gains: float32 [3, 256], replicated, may hold values from 0.6 to 10
- cross_qkv: bfloat16 [256, 768], replicated, may hold values from -0.45 to 0.45
- cross_out: bfloat16 [256, 256], replicated, may hold values from -0.375 to 0.375
- time_qkv: bfloat16 [256, 768], replicated, may hold values from -0.45 to 0.45
- time_out: bfloat16 [256, 256], replicated, may hold values from -0.375 to 0.375
- mlp_in: bfloat16 [256, 1024], replicated, may hold values from -0.375 to 0.375
- mlp_out: bfloat16 [1024, 256], replicated, may hold values from -0.1875 to 0.1875
Outputs:
- result: bfloat16 [4, 4, 8, 480, 256], P(('clips', 'view'), 'frame', 'rows'), parts along dimension 0
The draws below stay inside these ranges and needn't reach their ends.
There are 2 independent parts, one for each index of `clips`. The reference program is written for one: setup_inputs(seed, part) draws one part's arguments, and reference() takes and returns one part's arrays. A program takes and returns all parts, laid end to end along the dimension named above; an argument that names none is the same for every part. Nothing has to cross between parts.
All inputs are finite; a program needn't handle non-finite values.
Results may differ from the reference program's by a relative error of at most 0.012.
Values may be sent and summed in bfloat16 or wider, within the bound.
A program may use at most 64 MiB of HBM per device.

```python
import jax
import jax.numpy as jnp
from jax import lax

C = 256
HEADS = 8
FFN = 1024
W = 480
FRAMES = 4
H = 8


def draw_feats(key, part):
    subkeys = jax.random.split(key, 6)
    return jnp.clip(jax.random.normal(subkeys[5], (2, FRAMES, H, W, C), jnp.float32), -6.0, 6.0).astype(jnp.bfloat16)


def tied_weight(key):
    weight = jnp.clip(jax.random.normal(key, (C, 3 * C), jnp.float32), -6.0, 6.0) * C ** (-0.5)
    return jnp.clip(weight, -0.45, 0.45)


def draw_cross_qkv(key, part):
    return tied_weight(jax.random.fold_in(key, 11)).astype(jnp.bfloat16)


def draw_time_qkv(key, part):
    return tied_weight(jax.random.fold_in(key, 23)).astype(jnp.bfloat16)


def draw_norm_gains(key, part):
    subkeys = jax.random.split(key, 1)
    drawn = jax.random.uniform(subkeys[0], (3, C), jnp.float32, 0.6, 1.4)
    return drawn


def bell_draw(key, shape, scale, most, held_as=jnp.bfloat16):
    return jnp.clip(scale * jax.random.normal(key, shape, jnp.float32), -most, most).astype(held_as)


def setup_inputs(seed: int = 0, part: int = 0) -> dict:
    arg_keys = jax.random.split(jax.random.key(seed), 9)
    own_keys = jax.random.split(jax.random.fold_in(arg_keys[8], part), 9)
    return {
        "feats": draw_feats(jax.random.fold_in(jax.random.fold_in(arg_keys[8], part), 71), part),
        "norm_gains": draw_norm_gains(jax.random.fold_in(arg_keys[8], 71), part),
        "cross_qkv": draw_cross_qkv(jax.random.fold_in(arg_keys[8], 71), part),
        "cross_out": bell_draw(arg_keys[3], (C, C), C ** -0.5, 0.375),
        "time_qkv": draw_time_qkv(jax.random.fold_in(arg_keys[8], 71), part),
        "time_out": bell_draw(arg_keys[5], (C, C), C ** -0.5, 0.375),
        "mlp_in": bell_draw(arg_keys[6], (C, FFN), C ** -0.5, 0.375),
        "mlp_out": bell_draw(arg_keys[7], (FFN, C), FFN ** -0.5, 0.1875),
    }


EPSILON = 1e-05

def layer_norm(values, norm_gain):
    wide = values.astype(jnp.float32)
    centre = lax.optimization_barrier(jnp.mean(wide, axis=-1, keepdims=True))
    spread = lax.optimization_barrier(jnp.mean((wide - centre) ** 2, axis=-1, keepdims=True))
    return ((wide - centre) * lax.rsqrt(spread + EPSILON) * norm_gain).astype(jnp.bfloat16)

def row_attend(queries, key_rows, value_rows):
    length, channels = queries.shape
    head_dim = channels // HEADS
    q_heads = queries.astype(jnp.float32).reshape(length, HEADS, head_dim)
    k_heads = key_rows.astype(jnp.float32).reshape(length, HEADS, head_dim)
    v_heads = value_rows.astype(jnp.float32).reshape(length, HEADS, head_dim)
    scores = jnp.einsum('qhd,khd->hqk', q_heads, k_heads) * head_dim ** (-0.5)
    top_score = lax.optimization_barrier(jnp.max(scores, axis=-1, keepdims=True))
    expo = jnp.exp(scores - top_score)
    shares = (expo / lax.optimization_barrier(jnp.sum(expo, axis=-1, keepdims=True))).astype(jnp.bfloat16)
    mixed = jnp.einsum('hqk,khd->qhd', shares.astype(jnp.float32), v_heads)
    return mixed.reshape(length, channels).astype(jnp.bfloat16)

def time_attend(queries, key_rows, value_rows):
    frames, pixels, channels = queries.shape
    head_dim = channels // HEADS
    q_heads = queries.astype(jnp.float32).reshape(frames, pixels, HEADS, head_dim)
    k_heads = key_rows.astype(jnp.float32).reshape(frames, pixels, HEADS, head_dim)
    v_heads = value_rows.astype(jnp.float32).reshape(frames, pixels, HEADS, head_dim)
    scores = jnp.einsum('fnhd,gnhd->hfgn', q_heads, k_heads) * head_dim ** (-0.5)
    top_score = lax.optimization_barrier(jnp.max(scores, axis=2, keepdims=True))
    expo = jnp.exp(scores - top_score)
    shares = (expo / lax.optimization_barrier(jnp.sum(expo, axis=2, keepdims=True))).astype(jnp.bfloat16)
    mixed = jnp.einsum('hfgn,gnhd->fnhd', shares.astype(jnp.float32), v_heads)
    return mixed.reshape(frames, pixels, channels).astype(jnp.bfloat16)

def reference(feats, norm_gains, cross_qkv, cross_out, time_qkv, time_out, mlp_in, mlp_out):
    views, frames, height, row_width, channels = feats.shape
    tokens_flat = feats.reshape(-1, channels)
    normed_a = layer_norm(tokens_flat, norm_gains[0])
    projected = jnp.dot(normed_a, cross_qkv, preferred_element_type=jnp.float32).astype(jnp.bfloat16)
    projected = projected.reshape(views, frames * height, row_width, 3 * channels)
    queries = projected[..., :channels].reshape(-1, row_width, channels)
    partner = projected[::-1, :, :, channels:].reshape(-1, row_width, 2 * channels)

    def cross_row(pieces):
        return row_attend(pieces[0], pieces[1][:, :channels], pieces[1][:, channels:])
    cross_mix = lax.map(cross_row, (queries, partner)).reshape(-1, channels)
    stream_b = (tokens_flat.astype(jnp.float32) + jnp.dot(cross_mix, cross_out, preferred_element_type=jnp.float32)).astype(jnp.bfloat16)
    normed_b = layer_norm(stream_b, norm_gains[1])
    projected_t = jnp.dot(normed_b, time_qkv, preferred_element_type=jnp.float32).astype(jnp.bfloat16)
    projected_t = projected_t.reshape(views, frames, height, row_width, 3 * channels)
    regrouped = projected_t.transpose(0, 2, 1, 3, 4).reshape(views * height, frames, row_width, 3 * channels)

    def time_block(pixel_block):
        return time_attend(pixel_block[..., :channels], pixel_block[..., channels:2 * channels], pixel_block[..., 2 * channels:])
    time_mix = lax.map(time_block, regrouped).reshape(views, height, frames, row_width, channels)
    time_mix = time_mix.transpose(0, 2, 1, 3, 4).reshape(-1, channels)
    stream_c = (stream_b.astype(jnp.float32) + jnp.dot(time_mix, time_out, preferred_element_type=jnp.float32)).astype(jnp.bfloat16)
    normed_c = layer_norm(stream_c, norm_gains[2])
    inner_act = jax.nn.gelu(jnp.dot(normed_c, mlp_in, preferred_element_type=jnp.float32), approximate=True).astype(jnp.bfloat16)
    result = (stream_c.astype(jnp.float32) + jnp.dot(inner_act, mlp_out, preferred_element_type=jnp.float32)).astype(jnp.bfloat16)
    return result.reshape(feats.shape)
```

```python
import jax
import jax.numpy as jnp
from jax import lax
from jax.experimental import pallas as pl
from jax.experimental.pallas import tpu as pltpu
from jax.sharding import PartitionSpec as P

HEADS = 8


EPSILON = 1e-05


def swapped(value, axis, bit):
    return lax.ppermute(value, axis, [(i, i ^ 1 << bit) for i in range(lax.axis_size(axis))])


def layer_norm(values, norm_gain):
    wide = values.astype(jnp.float32)
    centre = jnp.mean(wide, axis=-1, keepdims=True)
    spread = jnp.mean((wide - centre) ** 2, axis=-1, keepdims=True)
    return ((wide - centre) * lax.rsqrt(spread + EPSILON) * norm_gain).astype(jnp.bfloat16)


def row_attend(queries, key_rows, value_rows):
    length, channels = queries.shape
    head_dim = channels // HEADS
    q_heads = queries.reshape(length, HEADS, head_dim)
    k_heads = key_rows.reshape(length, HEADS, head_dim)
    v_heads = value_rows.reshape(length, HEADS, head_dim)
    scores = jnp.einsum(
        "qhd,khd->hqk", q_heads, k_heads, preferred_element_type=jnp.float32
    ) * head_dim ** (-0.5)
    top_score = jnp.max(scores, axis=-1, keepdims=True)
    expo = jnp.exp(scores - top_score)
    shares = (expo / jnp.sum(expo, axis=-1, keepdims=True)).astype(jnp.bfloat16)
    mixed = jnp.einsum("hqk,khd->qhd", shares, v_heads, preferred_element_type=jnp.float32)
    return mixed.reshape(length, channels).astype(jnp.bfloat16)


def time_attend(queries, key_rows, value_rows):
    frames, pixels, channels = queries.shape
    head_dim = channels // HEADS
    q_heads = queries.reshape(frames, pixels, HEADS, head_dim)
    k_heads = key_rows.reshape(frames, pixels, HEADS, head_dim)
    v_heads = value_rows.reshape(frames, pixels, HEADS, head_dim)
    scores = jnp.einsum(
        "fnhd,gnhd->hfgn", q_heads, k_heads, preferred_element_type=jnp.float32
    ) * head_dim ** (-0.5)
    top_score = jnp.max(scores, axis=2, keepdims=True)
    expo = jnp.exp(scores - top_score)
    shares = (expo / jnp.sum(expo, axis=2, keepdims=True)).astype(jnp.bfloat16)
    mixed = jnp.einsum("hfgn,gnhd->fnhd", shares, v_heads, preferred_element_type=jnp.float32)
    return mixed.reshape(frames, pixels, channels).astype(jnp.bfloat16)

MESH = pl.DeviceIdType.MESH
LOG2E = 1.4426950408889634


def widened_norm(wide, gain):
    centre = jnp.mean(wide, axis=-1, keepdims=True)
    moved = wide - centre
    spread = jnp.mean(moved * moved, axis=-1, keepdims=True)
    return (moved * lax.rsqrt(spread + EPSILON) * gain).astype(jnp.bfloat16)


def head_mask(channels, head_dim, head):
    lanes = lax.broadcasted_iota(jnp.int32, (1, channels), 1)
    inside = (lanes >= head * head_dim) & (lanes < (head + 1) * head_dim)
    return jnp.where(inside, 1.0, 0.0).astype(jnp.bfloat16)


def f32_dot(a, b):
    return jnp.dot(a, b, preferred_element_type=jnp.float32)


def block_kernel(
    feats, gains, cross_qkv, cross_out, time_qkv, time_out, mlp_in, mlp_out,
    result,
    other, q_buf, k_buf, v_buf, acc_lo, acc_hi, stream_b, normed_b, arrived, t_proj, mixed, returned,
    view_send, view_recv, out_send, out_recv, back_send, back_recv,
):
    rows, width, channels = feats.shape
    frames = 4
    head_dim = channels // HEADS
    half_heads = HEADS // 2
    part = width // 2
    scale = head_dim ** (-0.5) * LOG2E
    me = lax.axis_index("frame")
    view = lax.axis_index("view")
    peers = [lax.rem(me + d, frames) for d in range(1, frames)]

    barrier = pltpu.get_barrier_semaphore()
    pl.semaphore_signal(barrier, inc=1, device_id={"view": 1 - view}, device_id_type=MESH)
    for peer in peers:
        pl.semaphore_signal(barrier, inc=1, device_id={"frame": peer}, device_id_type=MESH)
    pl.semaphore_wait(barrier, frames)

    def view_copy(row):
        return pltpu.make_async_remote_copy(
            src_ref=feats.at[row], dst_ref=other.at[row],
            send_sem=view_send.at[row], recv_sem=view_recv.at[row],
            device_id={"view": 1 - view}, device_id_type=MESH)

    def owner_of(row, side):
        first = 1 - lax.rem((row + 1) // 2, 2)
        return first if side == 0 else frames - 1 - first

    def out_copy(row, side, turn, source, target):
        return pltpu.make_async_remote_copy(
            src_ref=normed_b.at[row, side], dst_ref=arrived.at[turn, source],
            send_sem=out_send.at[row, side], recv_sem=out_recv.at[turn, source],
            device_id={"frame": target}, device_id_type=MESH)

    my_side = me // 2
    my_inner = lax.rem((me + 1) // 2, 2)

    def back_copy(turn, frame, row, side):
        return pltpu.make_async_remote_copy(
            src_ref=mixed.at[turn, frame], dst_ref=returned.at[row, side],
            send_sem=back_send.at[turn, frame], recv_sem=back_recv.at[row, side],
            device_id={"frame": frame}, device_id_type=MESH)

    for row in range(rows):
        view_copy(row).start()

    def cross_step(row):
        own = widened_norm(feats[row].astype(jnp.float32), gains[0:1])
        q_buf[...] = f32_dot(own, cross_qkv[:, :channels]).astype(jnp.bfloat16)
        view_copy(row).wait_recv()
        theirs = widened_norm(other[row].astype(jnp.float32), gains[0:1])
        k_buf[...] = f32_dot(theirs, cross_qkv[:, channels:2 * channels]).astype(jnp.bfloat16)
        v_buf[...] = f32_dot(theirs, cross_qkv[:, 2 * channels:]).astype(jnp.bfloat16)
        acc_lo[...] = jnp.zeros_like(acc_lo)
        acc_hi[...] = jnp.zeros_like(acc_hi)

        @pl.loop(0, half_heads)
        def _(head):
            masks = (head_mask(channels, head_dim, head), head_mask(channels, head_dim, head + half_heads))
            for low in range(0, width, TILE):
                for own_head, acc in ((0, acc_lo), (1, acc_hi)):
                    q_head = q_buf[low:low + TILE] * masks[own_head]
                    v_head = v_buf[...] * masks[own_head] + masks[1 - own_head]
                    scores = lax.dot_general(
                        q_head, k_buf[...], (((1,), (1,)), ((), ())), preferred_element_type=jnp.float32)
                    top = jnp.max(scores, axis=-1, keepdims=True)
                    expo = jnp.exp2((scores - top) * scale).astype(jnp.bfloat16)
                    acc[low:low + TILE] += f32_dot(expo, v_head)

        near = channels // 2
        mix = jnp.concatenate(
            [acc_lo[:, :near] / acc_lo[:, near:], acc_hi[:, near:] / acc_hi[:, :near]], axis=1
        ).astype(jnp.bfloat16)
        summed = (feats[row].astype(jnp.float32) + f32_dot(mix, cross_out[...])).astype(jnp.bfloat16)
        stream_b[row] = summed
        normed = widened_norm(summed.astype(jnp.float32), gains[1:2])
        turn = row // 2
        for side in range(2):
            normed_b[row, side] = normed[side * part:(side + 1) * part]
            owner = owner_of(row, side)

            @pl.when(owner != me)
            def _():
                out_copy(row, side, turn, me, owner).start()

            @pl.when(owner == me)
            def _():
                arrived[turn, me] = normed_b[row, side]

    def time_step(turn):
        for peer in peers:
            out_copy(0, 0, turn, peer, peer).wait_recv()
        for frame in range(frames):
            t_proj[frame] = f32_dot(arrived[turn, frame], time_qkv[...]).astype(jnp.bfloat16)
        down_c = lax.broadcasted_iota(jnp.int32, (channels, 128), 0)
        down_h = lax.broadcasted_iota(jnp.int32, (channels, 128), 1)
        gather = jnp.where(
            (down_c >= down_h * head_dim) & (down_c < (down_h + 1) * head_dim), 1.0, 0.0
        ).astype(jnp.bfloat16)
        up_h = lax.broadcasted_iota(jnp.int32, (128, channels), 0)
        up_c = lax.broadcasted_iota(jnp.int32, (128, channels), 1)
        spread = jnp.where(
            (up_c >= up_h * head_dim) & (up_c < (up_h + 1) * head_dim), 1.0, 0.0
        ).astype(jnp.bfloat16)

        @pl.loop(0, part // PIX)
        def _(block):
            span = pl.ds(pl.multiple_of(block * PIX, PIX), PIX)
            for frame in range(frames):
                query = t_proj[frame, span, :channels].astype(jnp.float32)
                scores = []
                for other_frame in range(frames):
                    product = query * t_proj[other_frame, span, channels:2 * channels].astype(jnp.float32)
                    high = product.astype(jnp.bfloat16)
                    low = (product - high.astype(jnp.float32)).astype(jnp.bfloat16)
                    scores.append(f32_dot(high, gather) + f32_dot(low, gather))
                top = jnp.maximum(jnp.maximum(scores[0], scores[1]), jnp.maximum(scores[2], scores[3]))
                expo = [jnp.exp2((s - top) * scale) for s in scores]
                total = 1.0 / (expo[0] + expo[1] + expo[2] + expo[3])
                mix = jnp.zeros((PIX, channels), jnp.float32)
                for other_frame in range(frames):
                    share = f32_dot((expo[other_frame] * total).astype(jnp.bfloat16), spread)
                    mix = mix + share * t_proj[other_frame, span, 2 * channels:].astype(jnp.float32)
                mixed[turn, frame, span] = mix.astype(jnp.bfloat16)

        row = 2 * turn + lax.rem(turn + 1 + my_inner, 2)
        for peer in peers:
            back_copy(turn, peer, row, my_side).start()
        returned[row, my_side] = mixed[turn, me]

    def mlp_step(row):
        for side in range(2):
            @pl.when(owner_of(row, side) != me)
            def _():
                back_copy(0, me, row, side).wait_recv()

            sl = slice(side * part, (side + 1) * part)
            summed = (
                stream_b[row, sl].astype(jnp.float32) + f32_dot(returned[row, side], time_out[...])
            ).astype(jnp.bfloat16)
            wide = summed.astype(jnp.float32)
            normed = widened_norm(wide, gains[2:3])
            act = jax.nn.gelu(f32_dot(normed, mlp_in[...]), approximate=True).astype(jnp.bfloat16)
            result[row, sl] = (wide + f32_dot(act, mlp_out[...])).astype(jnp.bfloat16)

    pl.loop(0, rows)(cross_step)
    pl.loop(0, 2)(time_step)
    pl.loop(0, rows)(mlp_step)

    @pl.loop(0, rows)
    def _(row):
        view_copy(row).wait_send()
        for side in range(2):
            @pl.when(owner_of(row, side) != me)
            def _():
                out_copy(row, side, 0, me, me).wait_send()

    for turn in range(2):
        for peer in peers:
            back_copy(turn, peer, 0, 0).wait_send()


TILE = 240
PIX = 48


def fused(feats, norm_gains, cross_qkv, cross_out, time_qkv, time_out, mlp_in, mlp_out):
    rows, width, channels = feats.shape[2:]
    part = width // 2
    bf16, f32 = jnp.bfloat16, jnp.float32
    dma = pltpu.SemaphoreType.DMA
    return pl.pallas_call(
        block_kernel,
        out_shape=jax.ShapeDtypeStruct((rows, width, channels), bf16),
        in_specs=[pl.BlockSpec(memory_space=pltpu.VMEM)] * 8,
        out_specs=pl.BlockSpec(memory_space=pltpu.VMEM),
        scratch_shapes=[
            pltpu.VMEM((rows, width, channels), bf16),
            pltpu.VMEM((width, channels), bf16),
            pltpu.VMEM((width, channels), bf16),
            pltpu.VMEM((width, channels), bf16),
            pltpu.VMEM((width, channels), f32),
            pltpu.VMEM((width, channels), f32),
            pltpu.VMEM((rows, width, channels), bf16),
            pltpu.VMEM((rows, 2, part, channels), bf16),
            pltpu.VMEM((2, 4, part, channels), bf16),
            pltpu.VMEM((4, part, 3 * channels), bf16),
            pltpu.VMEM((2, 4, part, channels), bf16),
            pltpu.VMEM((rows, 2, part, channels), bf16),
            dma((rows,)), dma((rows,)),
            dma((rows, 2)), dma((2, 4)),
            dma((2, 4)), dma((rows, 2)),
        ],
        compiler_params=pltpu.CompilerParams(
            collective_id=0, has_side_effects=True, vmem_limit_bytes=56 * 1024 * 1024),
        name="stereo_block",
    )(feats[0, 0], norm_gains, cross_qkv, cross_out, time_qkv, time_out, mlp_in, mlp_out)[None, None]


def local(feats, norm_gains, cross_qkv, cross_out, time_qkv, time_out, mlp_in, mlp_out):
    rows_here, row_width, channels = (feats.shape[2], feats.shape[3], feats.shape[4])
    frame_count = lax.axis_size("frame")
    if frame_count == 4 and rows_here == 4 and row_width == 2 * TILE and channels == 256:
        return fused(feats, norm_gains, cross_qkv, cross_out, time_qkv, time_out, mlp_in, mlp_out)
    tokens_flat = feats[0, 0].reshape(-1, channels)
    pixel_count = tokens_flat.shape[0]
    block_pixels = pixel_count // frame_count
    normed_a = layer_norm(tokens_flat, norm_gains[0])
    projected = jnp.dot(normed_a, cross_qkv, preferred_element_type=jnp.float32).astype(
        jnp.bfloat16
    )
    queries = projected[:, :channels]
    partner = swapped(projected[:, channels:], "view", 0)

    def cross_row(pieces):
        return row_attend(pieces[0], pieces[1][:, :channels], pieces[1][:, channels:])

    cross_mix = lax.map(
        cross_row,
        (
            queries.reshape(rows_here, row_width, channels),
            partner.reshape(rows_here, row_width, 2 * channels),
        ),
    )
    cross_mix = cross_mix.reshape(-1, channels)
    stream_b = (
        tokens_flat.astype(jnp.float32)
        + jnp.dot(cross_mix, cross_out, preferred_element_type=jnp.float32)
    ).astype(jnp.bfloat16)
    normed_b = layer_norm(stream_b, norm_gains[1])
    outgoing = normed_b.reshape(1, frame_count, block_pixels, channels)
    gathered = lax.all_to_all(outgoing, "frame", split_axis=1, concat_axis=0, tiled=True)[:, 0]
    frames, pixels, _ = gathered.shape
    projected_b = jnp.dot(
        gathered.reshape(-1, channels), time_qkv, preferred_element_type=jnp.float32
    ).astype(jnp.bfloat16)
    projected_b = projected_b.reshape(frames, pixels, 3 * channels)
    mixed = time_attend(
        projected_b[..., :channels],
        projected_b[..., channels : 2 * channels],
        projected_b[..., 2 * channels :],
    )
    time_mix = mixed[:, None]
    returned = lax.all_to_all(time_mix, "frame", split_axis=0, concat_axis=1, tiled=True).reshape(
        pixel_count, channels
    )
    stream_c = (
        stream_b.astype(jnp.float32)
        + jnp.dot(returned, time_out, preferred_element_type=jnp.float32)
    ).astype(jnp.bfloat16)
    normed_c = layer_norm(stream_c, norm_gains[2])
    inner_act = jax.nn.gelu(
        jnp.dot(normed_c, mlp_in, preferred_element_type=jnp.float32), approximate=True
    ).astype(jnp.bfloat16)
    result = (
        stream_c.astype(jnp.float32)
        + jnp.dot(inner_act, mlp_out, preferred_element_type=jnp.float32)
    ).astype(jnp.bfloat16)
    return result.reshape(1, 1, rows_here, row_width, channels)


def solution(mesh):
    placed = (P(("clips", "view"), "frame", "rows", None, None), P(), P(), P(), P(), P(), P(), P())
    return jax.shard_map(
        local,
        mesh=mesh,
        in_specs=placed,
        out_specs=P(("clips", "view"), "frame", "rows", None, None),
        check_vma=False,
    )
```

```python
import jax
import jax.numpy as jnp
from jax import lax
from jax.experimental import pallas as pl
from jax.experimental.pallas import tpu as pltpu
from jax.sharding import PartitionSpec as P

HEADS = 8


EPSILON = 1e-05


def swapped(value, axis, bit):
    return lax.ppermute(value, axis, [(i, i ^ 1 << bit) for i in range(lax.axis_size(axis))])


def layer_norm(values, norm_gain):
    wide = values.astype(jnp.float32)
    centre = jnp.mean(wide, axis=-1, keepdims=True)
    spread = jnp.mean((wide - centre) ** 2, axis=-1, keepdims=True)
    return ((wide - centre) * lax.rsqrt(spread + EPSILON) * norm_gain).astype(jnp.bfloat16)


def row_attend(queries, key_rows, value_rows):
    length, channels = queries.shape
    head_dim = channels // HEADS
    q_heads = queries.reshape(length, HEADS, head_dim)
    k_heads = key_rows.reshape(length, HEADS, head_dim)
    v_heads = value_rows.reshape(length, HEADS, head_dim)
    scores = jnp.einsum(
        "qhd,khd->hqk", q_heads, k_heads, preferred_element_type=jnp.float32
    ) * head_dim ** (-0.5)
    top_score = jnp.max(scores, axis=-1, keepdims=True)
    expo = jnp.exp(scores - top_score)
    shares = (expo / jnp.sum(expo, axis=-1, keepdims=True)).astype(jnp.bfloat16)
    mixed = jnp.einsum("hqk,khd->qhd", shares, v_heads, preferred_element_type=jnp.float32)
    return mixed.reshape(length, channels).astype(jnp.bfloat16)


def time_attend(queries, key_rows, value_rows):
    frames, pixels, channels = queries.shape
    head_dim = channels // HEADS
    q_heads = queries.reshape(frames, pixels, HEADS, head_dim)
    k_heads = key_rows.reshape(frames, pixels, HEADS, head_dim)
    v_heads = value_rows.reshape(frames, pixels, HEADS, head_dim)
    scores = jnp.einsum(
        "fnhd,gnhd->hfgn", q_heads, k_heads, preferred_element_type=jnp.float32
    ) * head_dim ** (-0.5)
    top_score = jnp.max(scores, axis=2, keepdims=True)
    expo = jnp.exp(scores - top_score)
    shares = (expo / jnp.sum(expo, axis=2, keepdims=True)).astype(jnp.bfloat16)
    mixed = jnp.einsum("hfgn,gnhd->fnhd", shares, v_heads, preferred_element_type=jnp.float32)
    return mixed.reshape(frames, pixels, channels).astype(jnp.bfloat16)

MESH = pl.DeviceIdType.MESH
LOG2E = 1.4426950408889634


def widened_norm(wide, gain):
    centre = jnp.mean(wide, axis=-1, keepdims=True)
    moved = wide - centre
    spread = jnp.mean(moved * moved, axis=-1, keepdims=True)
    return (moved * lax.rsqrt(spread + EPSILON) * gain).astype(jnp.bfloat16)


def head_mask(channels, head_dim, head):
    lanes = lax.broadcasted_iota(jnp.int32, (1, channels), 1)
    inside = (lanes >= head * head_dim) & (lanes < (head + 1) * head_dim)
    return jnp.where(inside, 1.0, 0.0).astype(jnp.bfloat16)


def f32_dot(a, b):
    return jnp.dot(a, b, preferred_element_type=jnp.float32)


def block_kernel(
    feats, gains, cross_qkv, cross_out, time_qkv, time_out, mlp_in, mlp_out,
    result,
    other, q_buf, k_buf, v_buf, acc_lo, acc_hi, stream_b, normed_b, arrived, t_proj, mixed, returned,
    view_send, view_recv, out_send, out_recv, back_send, back_recv,
):
    rows, width, channels = feats.shape
    frames = 4
    head_dim = channels // HEADS
    half_heads = HEADS // 2
    part = width // 2
    scale = head_dim ** (-0.5) * LOG2E
    me = lax.axis_index("frame")
    view = lax.axis_index("view")
    peers = [lax.rem(me + d, frames) for d in range(1, frames)]

    barrier = pltpu.get_barrier_semaphore()
    pl.semaphore_signal(barrier, inc=1, device_id={"view": 1 - view}, device_id_type=MESH)
    for peer in peers:
        pl.semaphore_signal(barrier, inc=1, device_id={"frame": peer}, device_id_type=MESH)
    pl.semaphore_wait(barrier, frames)

    def view_copy(row):
        return pltpu.make_async_remote_copy(
            src_ref=feats.at[row], dst_ref=other.at[row],
            send_sem=view_send.at[row], recv_sem=view_recv.at[row],
            device_id={"view": 1 - view}, device_id_type=MESH)

    def owner_of(row, side):
        first = 1 - lax.rem((row + 1) // 2, 2)
        return first if side == 0 else frames - 1 - first

    def out_copy(row, side, turn, source, target):
        return pltpu.make_async_remote_copy(
            src_ref=normed_b.at[row, side], dst_ref=arrived.at[turn, source],
            send_sem=out_send.at[row, side], recv_sem=out_recv.at[turn, source],
            device_id={"frame": target}, device_id_type=MESH)

    my_side = me // 2
    my_inner = lax.rem((me + 1) // 2, 2)

    def back_copy(turn, frame, row, side):
        return pltpu.make_async_remote_copy(
            src_ref=mixed.at[turn, frame], dst_ref=returned.at[row, side],
            send_sem=back_send.at[turn, frame], recv_sem=back_recv.at[row, side],
            device_id={"frame": frame}, device_id_type=MESH)

    for row in range(rows):
        view_copy(row).start()

    def cross_step(row):
        own = widened_norm(feats[row].astype(jnp.float32), gains[0:1])
        q_buf[...] = f32_dot(own, cross_qkv[:, :channels]).astype(jnp.bfloat16)
        view_copy(row).wait_recv()
        theirs = widened_norm(other[row].astype(jnp.float32), gains[0:1])
        k_buf[...] = f32_dot(theirs, cross_qkv[:, channels:2 * channels]).astype(jnp.bfloat16)
        v_buf[...] = f32_dot(theirs, cross_qkv[:, 2 * channels:]).astype(jnp.bfloat16)
        acc_lo[...] = jnp.zeros_like(acc_lo)
        acc_hi[...] = jnp.zeros_like(acc_hi)

        @pl.loop(0, half_heads, unroll=UNROLL)
        def _(head):
            masks = (head_mask(channels, head_dim, head), head_mask(channels, head_dim, head + half_heads))
            for low in range(0, width, TILE):
                for own_head, acc in ((0, acc_lo), (1, acc_hi)):
                    q_head = q_buf[low:low + TILE] * masks[own_head]
                    v_head = v_buf[...] * masks[own_head] + masks[1 - own_head]
                    scores = lax.dot_general(
                        q_head, k_buf[...], (((1,), (1,)), ((), ())), preferred_element_type=jnp.float32)
                    top = jnp.max(scores, axis=-1, keepdims=True)
                    expo = jnp.exp2((scores - top) * scale).astype(jnp.bfloat16)
                    acc[low:low + TILE] += f32_dot(expo, v_head)

        near = channels // 2
        mix = jnp.concatenate(
            [acc_lo[:, :near] / acc_lo[:, near:], acc_hi[:, near:] / acc_hi[:, :near]], axis=1
        ).astype(jnp.bfloat16)
        summed = (feats[row].astype(jnp.float32) + f32_dot(mix, cross_out[...])).astype(jnp.bfloat16)
        stream_b[row] = summed
        normed = widened_norm(summed.astype(jnp.float32), gains[1:2])
        turn = row // 2
        for side in range(2):
            normed_b[row, side] = normed[side * part:(side + 1) * part]
            owner = owner_of(row, side)

            @pl.when(owner != me)
            def _():
                out_copy(row, side, turn, me, owner).start()

            @pl.when(owner == me)
            def _():
                arrived[turn, me] = normed_b[row, side]

    def time_step(turn):
        for peer in peers:
            out_copy(0, 0, turn, peer, peer).wait_recv()
        for frame in range(frames):
            t_proj[frame] = f32_dot(arrived[turn, frame], time_qkv[...]).astype(jnp.bfloat16)
        down_c = lax.broadcasted_iota(jnp.int32, (channels, 128), 0)
        down_h = lax.broadcasted_iota(jnp.int32, (channels, 128), 1)
        gather = jnp.where(
            (down_c >= down_h * head_dim) & (down_c < (down_h + 1) * head_dim), 1.0, 0.0
        ).astype(jnp.bfloat16)
        up_h = lax.broadcasted_iota(jnp.int32, (128, channels), 0)
        up_c = lax.broadcasted_iota(jnp.int32, (128, channels), 1)
        spread = jnp.where(
            (up_c >= up_h * head_dim) & (up_c < (up_h + 1) * head_dim), 1.0, 0.0
        ).astype(jnp.bfloat16)

        @pl.loop(0, part // PIX)
        def _(block):
            span = pl.ds(pl.multiple_of(block * PIX, PIX), PIX)
            for frame in range(frames):
                query = t_proj[frame, span, :channels].astype(jnp.float32)
                product = jnp.concatenate(
                    [query * t_proj[g, span, channels:2 * channels].astype(jnp.float32) for g in range(frames)],
                    axis=0)
                high = product.astype(jnp.bfloat16)
                low = (product - high.astype(jnp.float32)).astype(jnp.bfloat16)
                stacked = f32_dot(high, gather) + f32_dot(low, gather)
                scores = [stacked[g * PIX:(g + 1) * PIX] for g in range(frames)]
                top = jnp.maximum(jnp.maximum(scores[0], scores[1]), jnp.maximum(scores[2], scores[3]))
                expo = [jnp.exp2((s - top) * scale) for s in scores]
                total = 1.0 / (expo[0] + expo[1] + expo[2] + expo[3])
                shares = jnp.concatenate([e * total for e in expo], axis=0).astype(jnp.bfloat16)
                wide_shares = f32_dot(shares, spread)
                mix = jnp.zeros((PIX, channels), jnp.float32)
                for g in range(frames):
                    mix = mix + wide_shares[g * PIX:(g + 1) * PIX] * t_proj[
                        g, span, 2 * channels:].astype(jnp.float32)
                mixed[turn, frame, span] = mix.astype(jnp.bfloat16)

        row = 2 * turn + lax.rem(turn + 1 + my_inner, 2)
        for peer in peers:
            back_copy(turn, peer, row, my_side).start()
        returned[row, my_side] = mixed[turn, me]

    def mlp_step(row):
        for side in range(2):
            @pl.when(owner_of(row, side) != me)
            def _():
                back_copy(0, me, row, side).wait_recv()

            sl = slice(side * part, (side + 1) * part)
            summed = (
                stream_b[row, sl].astype(jnp.float32) + f32_dot(returned[row, side], time_out[...])
            ).astype(jnp.bfloat16)
            wide = summed.astype(jnp.float32)
            normed = widened_norm(wide, gains[2:3])
            act = jax.nn.gelu(f32_dot(normed, mlp_in[...]), approximate=True).astype(jnp.bfloat16)
            result[row, sl] = (wide + f32_dot(act, mlp_out[...])).astype(jnp.bfloat16)

    pl.loop(0, rows)(cross_step)
    pl.loop(0, 2)(time_step)
    pl.loop(0, rows)(mlp_step)

    @pl.loop(0, rows)
    def _(row):
        view_copy(row).wait_send()
        for side in range(2):
            @pl.when(owner_of(row, side) != me)
            def _():
                out_copy(row, side, 0, me, me).wait_send()

    for turn in range(2):
        for peer in peers:
            back_copy(turn, peer, 0, 0).wait_send()


UNROLL = 4
TILE = 480
PIX = 240


def fused(feats, norm_gains, cross_qkv, cross_out, time_qkv, time_out, mlp_in, mlp_out):
    rows, width, channels = feats.shape[2:]
    part = width // 2
    bf16, f32 = jnp.bfloat16, jnp.float32
    dma = pltpu.SemaphoreType.DMA
    return pl.pallas_call(
        block_kernel,
        out_shape=jax.ShapeDtypeStruct((rows, width, channels), bf16),
        in_specs=[pl.BlockSpec(memory_space=pltpu.VMEM)] * 8,
        out_specs=pl.BlockSpec(memory_space=pltpu.VMEM),
        scratch_shapes=[
            pltpu.VMEM((rows, width, channels), bf16),
            pltpu.VMEM((width, channels), bf16),
            pltpu.VMEM((width, channels), bf16),
            pltpu.VMEM((width, channels), bf16),
            pltpu.VMEM((width, channels), f32),
            pltpu.VMEM((width, channels), f32),
            pltpu.VMEM((rows, width, channels), bf16),
            pltpu.VMEM((rows, 2, part, channels), bf16),
            pltpu.VMEM((2, 4, part, channels), bf16),
            pltpu.VMEM((4, part, 3 * channels), bf16),
            pltpu.VMEM((2, 4, part, channels), bf16),
            pltpu.VMEM((rows, 2, part, channels), bf16),
            dma((rows,)), dma((rows,)),
            dma((rows, 2)), dma((2, 4)),
            dma((2, 4)), dma((rows, 2)),
        ],
        compiler_params=pltpu.CompilerParams(
            collective_id=0, has_side_effects=True, vmem_limit_bytes=56 * 1024 * 1024),
        name="stereo_block",
    )(feats[0, 0], norm_gains, cross_qkv, cross_out, time_qkv, time_out, mlp_in, mlp_out)[None, None]


def local(feats, norm_gains, cross_qkv, cross_out, time_qkv, time_out, mlp_in, mlp_out):
    rows_here, row_width, channels = (feats.shape[2], feats.shape[3], feats.shape[4])
    frame_count = lax.axis_size("frame")
    if frame_count == 4 and rows_here == 4 and row_width == 480 and channels == 256:
        return fused(feats, norm_gains, cross_qkv, cross_out, time_qkv, time_out, mlp_in, mlp_out)
    tokens_flat = feats[0, 0].reshape(-1, channels)
    pixel_count = tokens_flat.shape[0]
    block_pixels = pixel_count // frame_count
    normed_a = layer_norm(tokens_flat, norm_gains[0])
    projected = jnp.dot(normed_a, cross_qkv, preferred_element_type=jnp.float32).astype(
        jnp.bfloat16
    )
    queries = projected[:, :channels]
    partner = swapped(projected[:, channels:], "view", 0)

    def cross_row(pieces):
        return row_attend(pieces[0], pieces[1][:, :channels], pieces[1][:, channels:])

    cross_mix = lax.map(
        cross_row,
        (
            queries.reshape(rows_here, row_width, channels),
            partner.reshape(rows_here, row_width, 2 * channels),
        ),
    )
    cross_mix = cross_mix.reshape(-1, channels)
    stream_b = (
        tokens_flat.astype(jnp.float32)
        + jnp.dot(cross_mix, cross_out, preferred_element_type=jnp.float32)
    ).astype(jnp.bfloat16)
    normed_b = layer_norm(stream_b, norm_gains[1])
    outgoing = normed_b.reshape(1, frame_count, block_pixels, channels)
    gathered = lax.all_to_all(outgoing, "frame", split_axis=1, concat_axis=0, tiled=True)[:, 0]
    frames, pixels, _ = gathered.shape
    projected_b = jnp.dot(
        gathered.reshape(-1, channels), time_qkv, preferred_element_type=jnp.float32
    ).astype(jnp.bfloat16)
    projected_b = projected_b.reshape(frames, pixels, 3 * channels)
    mixed = time_attend(
        projected_b[..., :channels],
        projected_b[..., channels : 2 * channels],
        projected_b[..., 2 * channels :],
    )
    time_mix = mixed[:, None]
    returned = lax.all_to_all(time_mix, "frame", split_axis=0, concat_axis=1, tiled=True).reshape(
        pixel_count, channels
    )
    stream_c = (
        stream_b.astype(jnp.float32)
        + jnp.dot(returned, time_out, preferred_element_type=jnp.float32)
    ).astype(jnp.bfloat16)
    normed_c = layer_norm(stream_c, norm_gains[2])
    inner_act = jax.nn.gelu(
        jnp.dot(normed_c, mlp_in, preferred_element_type=jnp.float32), approximate=True
    ).astype(jnp.bfloat16)
    result = (
        stream_c.astype(jnp.float32)
        + jnp.dot(inner_act, mlp_out, preferred_element_type=jnp.float32)
    ).astype(jnp.bfloat16)
    return result.reshape(1, 1, rows_here, row_width, channels)


def solution(mesh):
    placed = (P(("clips", "view"), "frame", "rows", None, None), P(), P(), P(), P(), P(), P(), P())
    return jax.shard_map(
        local,
        mesh=mesh,
        in_specs=placed,
        out_specs=P(("clips", "view"), "frame", "rows", None, None),
        check_vma=False,
    )
```
